32 devices in a mesh: row: 4 (over y, x), col: 8 (over z, core).
Axes of the slice: x: 2, y: 2, z: 4, core: 2. Of those that a mesh axis runs over, the one named last changes fastest.
Arguments:
- pair: bfloat16 [256, 256, 128], P('row', 'col'), may hold values from -6 to 6
- cotangent: bfloat16 [256, 256, 128], P('row', 'col'), may hold values from -6 to 6
- res_mask: int32 [256], replicated, may hold values 0 or 1
- chain: int32 [256], replicated, may hold values from 0 to 3, never falling along the last dimension, each value on 1 to 128 neighbouring positions
- ln_in_gain: float32 [128], replicated, may hold values from 0.5 to 1.5
- ln_in_bias: float32 [128], replicated, may hold values from -3 to 3
- w_proj: bfloat16 [128, 512], replicated, may hold values from -0.5 to 0.5
- w_gate: bfloat16 [128, 128], replicated, may hold values from -0.5 to 0.5
- chain_bias: float32 [128], replicated, may hold values from -4 to 4
- ln_out_gain: float32 [128], replicated, may hold values from 0.5 to 1.5
- ln_out_bias: float32 [128], replicated, may hold values from -3 to 3
- w_out: bfloat16 [128, 128], replicated, may hold values from -0.5 to 0.5
Outputs:
- grad_pair: bfloat16 [256, 256, 128], P('row', 'col')
- grad_proj: float32 [128, 512], replicated
- grad_gate: float32 [128, 128], replicated
- grad_out: float32 [128, 128], replicated
The draws below stay inside these ranges and needn't reach their ends.
Inputs may be any that keep to these rules, and one draw needn't show every extreme that they name: chain never decreases along the residues.
All inputs are finite; a program needn't handle non-finite values.
Results may differ from the reference program's by a relative error of at most 0.02.
Values may be sent and summed in bfloat16 or wider, within the bound.
A program may use at most 128 MiB of HBM per device.

```python
import math
import jax
import jax.numpy as jnp
import numpy as np
from jax import lax

C = 128
H = 128
ROWS_DEV = 64
N = 256


def place_ends(drawn, stream_key, least, largest):
    spot = [jax.random.randint(jax.random.fold_in(stream_key, axis), (), 0, length) for axis, length in enumerate(drawn.shape)]
    widest = drawn.shape.index(max(drawn.shape))
    beside = spot[:widest] + [(spot[widest] + 1) % drawn.shape[widest]] + spot[widest + 1:]
    return drawn.at[tuple(spot)].set(least).at[tuple(beside)].set(largest)


def levels(key, extent, cuts, low, top_value):
    factor_of, own = 1.0, jax.random.fold_in(key, 6)
    for position, shards_of in cuts:
        heights = jnp.exp(jax.random.uniform(jax.random.fold_in(own, position), (shards_of,), jnp.float32, low / len(cuts), top_value / len(cuts)))
        factor_of = factor_of * jnp.repeat(heights, extent[position] // shards_of).reshape([-1 if axis == position else 1 for axis in range(len(extent))])
    return factor_of


def profile(count, total, most, skew):
    loads = [(1 << 20) // math.isqrt(rank ** skew) + 1 for rank in range(2, count + 1)]
    rest, holding = total - most - (count - 1), [1] * (count - 1)
    while rest > 0:
        candidates = [i for i in range(count - 1) if holding[i] < most]
        whole, left = sum([loads[i] for i in candidates]), rest
        for i in candidates:
            addition = min(most - holding[i], max(1, left * loads[i] // whole), rest)
            holding[i] = holding[i] + addition
            rest = rest - addition
    return np.array([most] + holding)


def ragged_sizes(own_key, number_of, total, most, slope):
    if number_of == 2:
        one = jax.random.randint(own_key, (), max(1, total - most), min(most, total - 1) + 1)
        return jnp.stack([one, total - one])
    sizes = jnp.asarray(profile(number_of, total, most, slope), jnp.int32)
    couples = (number_of - 1) // 2
    donor, sink = sizes[1:1 + 2 * couples:2], sizes[2:2 + 2 * couples:2]
    room = jnp.minimum(donor - 1, most - sink)
    passed = jax.random.randint(jax.random.fold_in(own_key, 1), (couples,), 0, 1 << 20) % (room + 1)
    sizes = sizes.at[1:1 + 2 * couples:2].set(donor - passed).at[2:2 + 2 * couples:2].set(sink + passed)
    return sizes[jax.random.permutation(jax.random.fold_in(own_key, 2), number_of)]


def gaussian(own_key, dims, deviation, reach, cuts=(), held_as=jnp.bfloat16):
    entries = deviation * jax.random.normal(own_key, dims, jnp.float32)
    if cuts:
        entries = entries * levels(own_key, dims, cuts, -0.22, 0.18)
    return jnp.clip(entries, -reach, reach).astype(held_as)


def setup_inputs(seed: int = 0) -> dict:
    key_of = jax.random.split(jax.random.key(seed), 13)
    return {
        "pair": gaussian(key_of[0], (N, N, C), 1.0, 6.0, ((0, 4), (1, 8))),
        "cotangent": gaussian(key_of[1], (N, N, C), 1.0, 6.0, ((0, 4), (1, 8))),
        "res_mask": place_ends((jax.random.randint(key_of[2], (N,), 0, 8) < 7).astype(jnp.int32), jax.random.fold_in(key_of[2], 1), 0, 1),
        "chain": jnp.searchsorted(jnp.cumsum(ragged_sizes(key_of[3], 4, N, N // 2, 1)), jnp.arange(N), side="right").astype(jnp.int32),
        "ln_in_gain": jnp.clip(1.0 + 0.1 * jax.random.normal(key_of[4], (C,), jnp.float32), 0.5, 1.5),
        "ln_in_bias": gaussian(key_of[5], (C,), 0.5, 3.0, (), jnp.float32),
        "w_proj": gaussian(key_of[6], (C, 4 * H), C ** -0.5, 0.5),
        "w_gate": gaussian(key_of[7], (C, C), C ** -0.5, 0.5),
        "chain_bias": gaussian(key_of[8], (C,), 1.0, 4.0, (), jnp.float32),
        "ln_out_gain": jnp.clip(1.0 + 0.1 * jax.random.normal(key_of[9], (H,), jnp.float32), 0.5, 1.5),
        "ln_out_bias": gaussian(key_of[10], (H,), 0.5, 3.0, (), jnp.float32),
        "w_out": gaussian(key_of[11], (H, C), H ** -0.5, 0.5),
    }


EPS = 1e-05

def layer_norm(values, gain, bias):
    mean = lax.optimization_barrier(jnp.mean(values, axis=-1, keepdims=True))
    centred = values - mean
    inverse = lax.rsqrt(lax.optimization_barrier(jnp.mean(centred * centred, axis=-1, keepdims=True)) + EPS)
    normed = centred * inverse
    return (normed * gain + bias, normed, inverse)

def norm_back(grad_normed, normed, inverse):
    first = lax.optimization_barrier(jnp.mean(grad_normed, axis=-1, keepdims=True))
    second = lax.optimization_barrier(jnp.mean(grad_normed * normed, axis=-1, keepdims=True))
    return (grad_normed - first - normed * second) * inverse

def matmul_last(left, right):
    shape = left.shape
    flat = jnp.dot(left.reshape(-1, shape[-1]), right, preferred_element_type=jnp.float32)
    return flat.reshape(shape[:-1] + (right.shape[1],))

def contract_pairs(left, right):
    flat_left = left.reshape(-1, left.shape[-1])
    flat_right = right.reshape(-1, right.shape[-1])
    return lax.dot_general(flat_left, flat_right, (((0,), (0,)), ((), ())), preferred_element_type=jnp.float32)

def project(pair, ln_in_gain, ln_in_bias, w_proj):
    scaled, normed, inverse = layer_norm(pair.astype(jnp.float32), ln_in_gain, ln_in_bias)
    normed_b = scaled.astype(jnp.bfloat16)
    return (normed_b, normed, inverse, matmul_last(normed_b, w_proj))

def activations(proj, pair_mask):
    width = proj.shape[-1] // 4
    gate_a = jax.nn.sigmoid(proj[..., :width])
    gate_b = jax.nn.sigmoid(proj[..., 2 * width:3 * width])
    act_a = (gate_a * proj[..., width:2 * width] * pair_mask).astype(jnp.bfloat16)
    act_b = (gate_b * proj[..., 3 * width:] * pair_mask).astype(jnp.bfloat16)
    return (act_a, act_b)

def gated_output(mixed, cotangent, normed_b, same, chain_bias, w_gate, ln_out_gain, ln_out_bias, w_out):
    scaled, normed, inverse = layer_norm(mixed, ln_out_gain, ln_out_bias)
    out_b = scaled.astype(jnp.bfloat16)
    update = matmul_last(out_b, w_out)
    gate = jax.nn.sigmoid(matmul_last(normed_b, w_gate) + same * chain_bias)
    cot = cotangent.astype(jnp.float32)
    grad_update = (cot * gate).astype(jnp.bfloat16)
    grad_logit = (cot * update * gate * (1.0 - gate)).astype(jnp.bfloat16)
    grad_scaled = matmul_last(grad_update, w_out.T)
    grad_mixed = norm_back(grad_scaled * ln_out_gain, normed, inverse).astype(jnp.bfloat16)
    return (grad_mixed, grad_logit, contract_pairs(out_b, grad_update), contract_pairs(normed_b, grad_logit))

def input_back(normed_b, normed, inverse, proj, pair_mask, grad_a, grad_b, grad_logit, ln_in_gain, w_proj, w_gate):
    width = proj.shape[-1] // 4
    gate_a = jax.nn.sigmoid(proj[..., :width])
    gate_b = jax.nn.sigmoid(proj[..., 2 * width:3 * width])
    masked_a = grad_a * pair_mask
    masked_b = grad_b * pair_mask
    grad_p = jnp.concatenate([masked_a * proj[..., width:2 * width] * gate_a * (1.0 - gate_a), masked_a * gate_a, masked_b * proj[..., 3 * width:] * gate_b * (1.0 - gate_b), masked_b * gate_b], axis=-1).astype(jnp.bfloat16)
    grad_zn = matmul_last(grad_p, w_proj.T) + matmul_last(grad_logit, w_gate.T)
    grad_pair = norm_back(grad_zn * ln_in_gain, normed, inverse).astype(jnp.bfloat16)
    return (grad_pair, contract_pairs(normed_b, grad_p))

def reference(pair, cotangent, res_mask, chain, ln_in_gain, ln_in_bias, w_proj, w_gate, chain_bias, ln_out_gain, ln_out_bias, w_out):
    blocks = N // ROWS_DEV
    maskf = res_mask.astype(jnp.float32)

    def split(values):
        return values.reshape((blocks, ROWS_DEV) + values.shape[1:])

    def first(items):
        pair_rows, mask_rows = items
        pair_mask = mask_rows[:, None, None] * maskf[None, :, None]
        proj = project(pair_rows, ln_in_gain, ln_in_bias, w_proj)[3]
        return activations(proj, pair_mask)
    act_a, act_b = lax.map(first, (split(pair), split(maskf)))
    act_a = act_a.reshape(N, N, H)
    act_b = act_b.reshape(N, N, H)
    mixed = jnp.einsum('ikh,jkh->ijh', act_a.astype(jnp.float32), act_b.astype(jnp.float32))

    def second(items):
        mixed_rows, cot_rows, pair_rows, chain_rows = items
        normed_b = project(pair_rows, ln_in_gain, ln_in_bias, w_proj)[0]
        same = (chain_rows[:, None] == chain[None, :]).astype(jnp.float32)[:, :, None]
        return gated_output(mixed_rows, cot_rows, normed_b, same, chain_bias, w_gate, ln_out_gain, ln_out_bias, w_out)
    grad_mixed, grad_logit, terms_out, terms_gate = lax.map(second, (split(mixed), split(cotangent), split(pair), split(chain)))
    grad_mixed = grad_mixed.reshape(N, N, H)
    grad_a = jnp.einsum('ijh,jkh->ikh', grad_mixed.astype(jnp.float32), act_b.astype(jnp.float32))
    grad_b = jnp.einsum('ijh,ikh->jkh', grad_mixed.astype(jnp.float32), act_a.astype(jnp.float32))

    def third(items):
        pair_rows, mask_rows, grad_a_rows, grad_b_rows, logit_rows = items
        pair_mask = mask_rows[:, None, None] * maskf[None, :, None]
        normed_b, normed, inverse, proj = project(pair_rows, ln_in_gain, ln_in_bias, w_proj)
        return input_back(normed_b, normed, inverse, proj, pair_mask, grad_a_rows, grad_b_rows, logit_rows, ln_in_gain, w_proj, w_gate)
    grad_pair, terms_proj = lax.map(third, (split(pair), split(maskf), split(grad_a), split(grad_b), grad_logit))
    scale = 1.0 / N
    return (grad_pair.reshape(N, N, C), lax.optimization_barrier(jnp.sum(terms_proj, axis=0)) * scale, lax.optimization_barrier(jnp.sum(terms_gate, axis=0)) * scale, lax.optimization_barrier(jnp.sum(terms_out, axis=0)) * scale)
```

```python
import functools

import jax
import jax.numpy as jnp
from jax import lax
from jax.experimental import pallas as pl
from jax.experimental.pallas import tpu as pltpu
from jax.sharding import PartitionSpec as P

EPS = 1e-05
MESH = pl.DeviceIdType.MESH
F32 = jnp.float32
BF16 = jnp.bfloat16
LANES = 128


def dot(left, right, dims):
    return lax.dot_general(left, right, ((dims[:1], dims[1:]), ((), ())), preferred_element_type=F32)


def mean(values):
    return jnp.mean(values, axis=-1, keepdims=True)


def normalise(values):
    centred = values - mean(values)
    inverse = lax.rsqrt(mean(centred * centred) + EPS)
    return centred * inverse, inverse


def norm_back(grad, normed, inverse):
    return (grad - mean(grad) - normed * mean(grad * normed)) * inverse


def unfold(values, rows):
    parts = values.reshape(-1, 16, LANES)
    return jnp.concatenate([parts[:, :, :rows], parts[:, :, rows:]], axis=1).reshape(-1, rows)


def fold(values, rows):
    parts = values.reshape(-1, 32, rows)
    return jnp.concatenate([parts[:, :16], parts[:, 16:]], axis=2).reshape(-1, LANES)


def kernel(
    nr, nc, rows, cols,
    pair, cot, mask_s, chain_s, mask_v, chain_v, gain_in, bias_in, w_proj, w_gate, chain_bias,
    gain_out, bias_out, w_out,
    out, out_proj, out_gate, out_out,
    in32, cot32, zn_s, normed_s, inv_s, act_s, gate_s, y_s, gu_s, gl_s, gz_s,
    fold_a, fold_b, big32, a_mats, b_mats, g_mats,
    a_send, a_recv, b_send, b_all, m_send, m_recv, g_send, g_recv, ga_send, ga_recv,
    gp_send, gp_recv, gb_send, gb_recv, acc, w_send, w_recv, r_recv, f_recv,
    send_sem, recv_sem, bs_sem, br_sem, ps_sem, pr_sem, rs_sem, rr_sem,
):
    r = lax.axis_index("row")
    c = lax.axis_index("col")
    total = nr * rows
    hc = LANES // nc
    slab = 16 * hc
    full = nc * slab
    steps = 16
    lines = nc * 16

    def mod(value, count):
        return lax.rem(value + count, count)

    def at(ref, start, size):
        return ref.at[pl.ds(pl.multiple_of(start, 16), size)]

    barrier = pltpu.get_barrier_semaphore()
    for o in range(1, nc):
        pl.semaphore_signal(barrier, inc=1, device_id=(r, mod(c + o, nc)), device_id_type=MESH)
    for o in range(1, nr):
        pl.semaphore_signal(barrier, inc=1, device_id=(mod(r + o, nr), c), device_id_type=MESH)

    def col_copy(which, o, src, dst):
        return pltpu.make_async_remote_copy(
            src_ref=src, dst_ref=dst, send_sem=send_sem.at[which, o], recv_sem=recv_sem.at[which, o],
            device_id=(r, mod(c + o, nc)), device_id_type=MESH)

    def scatter(which, src, dst, base=0, size=slab):
        for o in range(1, nc):
            col_copy(which, o, at(src, mod(c + o, nc) * size, size), at(dst, base + c * size, size)).start()
        own = pl.ds(pl.multiple_of(base + c * size, 16), size)
        dst[own, :] = src[pl.ds(pl.multiple_of(c * size, 16), size), :]

    def arrived(which, o, src, dst, base=0, size=slab):
        col_copy(which, o, at(src, 0, size), at(dst, base + mod(c - o, nc) * size, size)).wait_recv()

    def gathered(which, src, dst, base=0, size=slab):
        for o in range(1, nc):
            arrived(which, o, src, dst, base, size)

    def cast(dst, src, count):
        size = 256
        def step(t, carry):
            part = pl.ds(pl.multiple_of(t * size, size), size)
            dst[part, :] = src[part, :].astype(dst.dtype)
            return carry
        lax.fori_loop(0, count // size, step, 0)

    def put_turned(dst, low, values):
        turned = values.T
        for t in range(nc):
            dst[pl.ds(pl.multiple_of((t * 16 + low) * hc, hc), hc), :] = turned[t * hc:(t + 1) * hc]

    def get_turned(src, low):
        parts = [src[pl.ds(pl.multiple_of((t * 16 + low) * hc, hc), hc), :] for t in range(nc)]
        return jnp.concatenate(parts, axis=0).T

    def natural(src, low):
        return jnp.concatenate([src[pl.ds(low, rows, stride=cols), :], src[pl.ds(low + 16, rows, stride=cols), :]], axis=0)

    def here(low):
        return pl.ds(pl.multiple_of(low * LANES, LANES), LANES)

    upper = lax.broadcasted_iota(jnp.int32, (LANES, 1), 0) >= rows
    mask_rows = mask_v[pl.ds(pl.multiple_of(r * rows, rows), rows), :].astype(F32)
    mask_rows = jnp.concatenate([mask_rows, mask_rows], axis=0)
    chain_rows = chain_v[pl.ds(pl.multiple_of(r * rows, rows), rows), :]
    chain_rows = jnp.concatenate([chain_rows, chain_rows], axis=0)

    def pair_mask(low):
        first = mask_s[c * cols + low].astype(F32)
        second = mask_s[c * cols + low + 16].astype(F32)
        return mask_rows * jnp.where(upper, second, first)

    cast(in32, pair, rows * cols)

    def project(low, carry):
        normed, inverse = normalise(natural(in32, low))
        zn = (normed * gain_in[...] + bias_in[...]).astype(BF16)
        zn_s[here(low), :] = zn
        normed_s[here(low), :] = normed
        inv_s[here(low), :] = inverse
        proj = dot(zn, w_proj[...], (1, 0))
        mask = pair_mask(low)
        gate_a = jax.nn.sigmoid(proj[:, :LANES])
        gate_b = jax.nn.sigmoid(proj[:, 2 * LANES:3 * LANES])
        value_a = proj[:, LANES:2 * LANES]
        value_b = proj[:, 3 * LANES:]
        act_s[here(low), :LANES] = gate_a
        act_s[here(low), LANES:2 * LANES] = value_a
        act_s[here(low), 2 * LANES:3 * LANES] = gate_b
        act_s[here(low), 3 * LANES:] = value_b
        put_turned(fold_a, low, gate_a * value_a * mask)
        put_turned(fold_b, low, gate_b * value_b * mask)
        return carry

    lax.fori_loop(0, steps, project, 0)
    cast(b_send, fold_b, full)
    cast(a_send, fold_a, full)
    pl.semaphore_wait(barrier, nc - 1 + nr - 1)

    def row_copy(sems, o, slot, src, dst):
        return pltpu.make_async_remote_copy(
            src_ref=src, dst_ref=dst, send_sem=sems[0].at[o, slot], recv_sem=sems[1].at[o, slot],
            device_id=(mod(r + o, nr), c), device_id_type=MESH)

    b_base = r * full
    scatter(0, b_send, b_all, b_base)
    scatter(1, a_send, a_recv)

    def spread(slot):
        piece = at(b_all, b_base + mod(c - slot, nc) * slab, slab)
        for o in range(1, nr):
            row_copy((bs_sem, br_sem), o, slot, piece, piece).start()

    spread(0)
    for slot in range(1, nc):
        arrived(0, slot, b_send, b_all, b_base)
        spread(slot)

    cast(cot32, cot, rows * cols)

    def gates(low, carry):
        first = chain_s[c * cols + low]
        second = chain_s[c * cols + low + 16]
        same = (chain_rows == jnp.where(upper, second, first)).astype(F32)
        logit = dot(zn_s[here(low), :], w_gate[...], (1, 0)) + same * chain_bias[...]
        gate_s[here(low), :] = jax.nn.sigmoid(logit)
        return carry

    lax.fori_loop(0, steps, gates, 0)

    gathered(1, a_send, a_recv)
    cast(fold_a, a_recv, full)
    for slot in range(nc):
        for o in range(1, nr):
            piece = at(b_all, mod(r - o, nr) * full + mod(c - slot, nc) * slab, slab)
            row_copy((bs_sem, br_sem), o, slot, piece, piece).wait_recv()
    cast(big32, b_all, nr * full)

    def mix(h, carry):
        a_mat = unfold(fold_a[pl.ds(h, lines, stride=hc), :], rows).astype(BF16)
        b_mat = jnp.concatenate(
            [unfold(big32[pl.ds(t * full + h, lines, stride=hc), :], rows) for t in range(nr)], axis=1
        ).astype(BF16)
        a_mats[h] = a_mat
        b_mats[h] = b_mat
        fold_b[pl.ds(h, lines, stride=hc), :] = fold(dot(b_mat, a_mat, (0, 0)), rows)
        return carry

    lax.fori_loop(0, hc, mix, 0)
    cast(m_send, fold_b, full)
    scatter(2, m_send, m_recv)
    acc[...] = jnp.zeros_like(acc)
    gathered(2, m_send, m_recv)
    cast(fold_a, m_recv, full)

    def middle(low, carry):
        normed, inverse = normalise(get_turned(fold_a, low))
        y = (normed * gain_out[...] + bias_out[...]).astype(BF16)
        update = dot(y, w_out[...], (1, 0))
        gate = gate_s[here(low), :]
        cot_here = natural(cot32, low)
        grad_update = (cot_here * gate).astype(BF16)
        y_s[here(low), :] = y
        gu_s[here(low), :] = grad_update
        gl_s[here(low), :] = (cot_here * update * gate * (1.0 - gate)).astype(BF16)
        grad_y = dot(grad_update, w_out[...], (1, 1))
        put_turned(fold_b, low, norm_back(grad_y * gain_out[...], normed, inverse))
        return carry

    lax.fori_loop(0, steps, middle, 0)
    cast(g_send, fold_b, full)
    scatter(3, g_send, g_recv)

    def side_terms(low, carry):
        acc[4 * LANES:5 * LANES, :] += dot(zn_s[here(low), :], gl_s[here(low), :], (0, 0))
        acc[5 * LANES:, :] += dot(y_s[here(low), :], gu_s[here(low), :], (0, 0))
        gz_s[here(low), :] = dot(gl_s[here(low), :], w_gate[...], (1, 1))
        return carry

    lax.fori_loop(0, steps, side_terms, 0)
    gathered(3, g_send, g_recv)
    cast(fold_a, g_recv, full)

    def back_b(h, carry):
        g_mat = unfold(fold_a[pl.ds(h, lines, stride=hc), :], rows).astype(BF16)
        g_mats[h] = g_mat
        grad = dot(a_mats[h], g_mat, (1, 1))
        for t in range(nr):
            big32[pl.ds(t * full + h, lines, stride=hc), :] = fold(grad[:, t * rows:(t + 1) * rows], rows)
        return carry

    lax.fori_loop(0, hc, back_b, 0)
    cast(gp_send, big32, nr * full)
    for slot in range(nc):
        for o in range(1, nr):
            src = at(gp_send, mod(r + o, nr) * full + mod(c + slot, nc) * slab, slab)
            dst = at(gp_recv, o * full + slot * slab, slab)
            row_copy((ps_sem, pr_sem), o, slot, src, dst).start()

    def back_a(h, carry):
        fold_b[pl.ds(h, lines, stride=hc), :] = fold(dot(b_mats[h], g_mats[h], (1, 0)), rows)
        return carry

    lax.fori_loop(0, hc, back_a, 0)
    cast(ga_send, fold_b, full)
    scatter(4, ga_send, ga_recv)

    for slot in list(range(1, nc)) + [0]:
        target = mod(c + slot, nc) * slab
        summed = big32[pl.ds(pl.multiple_of(r * full + target, 16), slab), :]
        for o in range(1, nr):
            piece = at(gp_recv, o * full + slot * slab, slab)
            row_copy((ps_sem, pr_sem), o, slot, piece, piece).wait_recv()
            summed = summed + gp_recv[pl.ds(o * full + slot * slab, slab), :].astype(F32)
        if slot == 0:
            gb_recv[pl.ds(pl.multiple_of(c * slab, 16), slab), :] = summed.astype(BF16)
        else:
            gb_send[pl.ds(pl.multiple_of(target, 16), slab), :] = summed.astype(BF16)
            col_copy(5, slot, at(gb_send, target, slab), at(gb_recv, c * slab, slab)).start()

    def half(low, src, gate_at, block):
        masked = get_turned(src, low) * pair_mask(low)
        gate = act_s[here(low), gate_at:gate_at + LANES]
        value = act_s[here(low), gate_at + LANES:gate_at + 2 * LANES]
        value_grad = masked * gate
        grad_p = jnp.concatenate([value_grad * value * (1.0 - gate), value_grad], axis=1).astype(BF16)
        term = dot(zn_s[here(low), :], grad_p, (0, 0))
        acc[block * LANES:(block + 1) * LANES, :] += term[:, :LANES]
        acc[(block + 1) * LANES:(block + 2) * LANES, :] += term[:, LANES:]
        return gz_s[here(low), :] + dot(grad_p, w_proj[:, gate_at:gate_at + 2 * LANES], (1, 1))

    gathered(4, ga_send, ga_recv)
    cast(fold_a, ga_recv, full)

    def finish_a(low, carry):
        gz_s[here(low), :] = half(low, fold_a, 0, 0)
        return carry

    lax.fori_loop(0, steps, finish_a, 0)
    gathered(5, gb_send, gb_recv)
    cast(fold_b, gb_recv, full)

    def finish_b(low, carry):
        grad = half(low, fold_b, 2 * LANES, 2) * gain_in[...]
        result = norm_back(grad, normed_s[here(low), :], inv_s[here(low), :])
        in32[pl.ds(low, rows, stride=cols), :] = result[:rows]
        in32[pl.ds(low + 16, rows, stride=cols), :] = result[rows:]
        return carry

    lax.fori_loop(0, steps, finish_b, 0)

    share = 6 * LANES // nc
    cast(w_send, acc, 6 * LANES)
    scatter(6, w_send, w_recv, 0, share)
    cast(out, in32, rows * cols)
    gathered(6, w_send, w_recv, 0, share)
    part = w_recv[:share, :].astype(F32)
    for t in range(1, nc):
        part = part + w_recv[t * share:(t + 1) * share, :].astype(F32)
    mine = pl.ds(pl.multiple_of(r * share, 16), share)
    r_recv[mine, :] = part.astype(BF16)
    for o in range(1, nr):
        piece = at(r_recv, r * share, share)
        row_copy((rs_sem, rr_sem), o, 0, piece, piece).start()
    for o in range(1, nr):
        piece = at(r_recv, mod(r - o, nr) * share, share)
        row_copy((rs_sem, rr_sem), o, 0, piece, piece).wait_recv()
    part = r_recv[:share, :].astype(F32)
    for t in range(1, nr):
        part = part + r_recv[t * share:(t + 1) * share, :].astype(F32)
    f_recv[pl.ds(pl.multiple_of(c * share, 16), share), :] = (part * (1.0 / total)).astype(BF16)
    for o in range(1, nc):
        piece = at(f_recv, c * share, share)
        col_copy(7, o, piece, piece).start()
    gathered(7, f_recv, f_recv, 0, share)
    for t in range(4):
        out_proj[:, t * LANES:(t + 1) * LANES] = f_recv[t * LANES:(t + 1) * LANES, :].astype(F32)
    out_gate[...] = f_recv[4 * LANES:5 * LANES, :].astype(F32)
    out_out[...] = f_recv[5 * LANES:, :].astype(F32)

    for o in range(1, nc):
        for which, ref, size in (
            (0, b_send, slab), (1, a_send, slab), (2, m_send, slab), (3, g_send, slab),
            (4, ga_send, slab), (5, gb_send, slab), (6, w_send, share), (7, f_recv, share),
        ):
            col_copy(which, o, at(ref, 0, size), at(ref, 0, size)).wait_send()
    for o in range(1, nr):
        for slot in range(nc):
            row_copy((bs_sem, br_sem), o, slot, at(b_all, 0, slab), at(b_all, 0, slab)).wait_send()
            row_copy((ps_sem, pr_sem), o, slot, at(gp_send, 0, slab), at(gp_send, 0, slab)).wait_send()
        row_copy((rs_sem, rr_sem), o, 0, at(r_recv, 0, share), at(r_recv, 0, share)).wait_send()


def body(
    nr, nc, pair, cotangent, res_mask, chain, ln_in_gain, ln_in_bias, w_proj, w_gate, chain_bias,
    ln_out_gain, ln_out_bias, w_out,
):
    rows, cols, width = pair.shape
    count = rows * cols
    total = nr * rows
    hc = LANES // nc
    full = LANES * 16
    share = 6 * LANES // nc
    vmem = pl.BlockSpec(memory_space=pltpu.VMEM)
    smem = pl.BlockSpec(memory_space=pltpu.SMEM)

    def wide(size, dtype=BF16):
        return pltpu.VMEM((size, LANES), dtype)

    scratch = [
        wide(count, F32), wide(count, F32), wide(count), wide(count, F32), pltpu.VMEM((count, 1), F32),
        pltpu.VMEM((count, 4 * LANES), F32), wide(count, F32), wide(count), wide(count), wide(count), wide(count, F32),
        wide(full, F32), wide(full, F32), wide(nr * full, F32),
        pltpu.VMEM((hc, total, rows), BF16), pltpu.VMEM((hc, total, total), BF16), pltpu.VMEM((hc, total, rows), BF16),
        wide(full), wide(full), wide(full), wide(nr * full), wide(full), wide(full), wide(full), wide(full), wide(full), wide(full),
        wide(nr * full), wide(nr * full), wide(full), wide(full), wide(6 * LANES, F32),
        wide(6 * LANES), wide(6 * LANES), wide(nr * share), wide(6 * LANES),
        pltpu.SemaphoreType.DMA((8, nc)), pltpu.SemaphoreType.DMA((8, nc)),
        pltpu.SemaphoreType.DMA((nr, nc)), pltpu.SemaphoreType.DMA((nr, nc)),
        pltpu.SemaphoreType.DMA((nr, nc)), pltpu.SemaphoreType.DMA((nr, nc)),
        pltpu.SemaphoreType.DMA((nr, 1)), pltpu.SemaphoreType.DMA((nr, 1)),
    ]
    row = lambda values: values.reshape(1, -1)
    grads = pl.pallas_call(
        functools.partial(kernel, nr, nc, rows, cols),
        out_shape=(
            jax.ShapeDtypeStruct((count, width), BF16),
            jax.ShapeDtypeStruct((width, 4 * LANES), F32),
            jax.ShapeDtypeStruct((width, width), F32),
            jax.ShapeDtypeStruct((LANES, width), F32),
        ),
        in_specs=[vmem, vmem, smem, smem] + [vmem] * 10,
        out_specs=(vmem,) * 4,
        scratch_shapes=scratch,
        compiler_params=pltpu.CompilerParams(collective_id=0, has_side_effects=True, vmem_limit_bytes=56 * 2**20),
        cost_estimate=pl.CostEstimate(flops=2 * 10**9, bytes_accessed=4 * 2**20, transcendentals=0),
    )(
        pair.reshape(count, width), cotangent.reshape(count, width), res_mask, chain,
        res_mask.reshape(-1, 1), chain.reshape(-1, 1), row(ln_in_gain), row(ln_in_bias), w_proj, w_gate,
        row(chain_bias), row(ln_out_gain), row(ln_out_bias), w_out,
    )
    return (grads[0].reshape(rows, cols, width),) + tuple(grads[1:])


def solution(mesh):
    split = P("row", "col", None)
    return jax.shard_map(
        functools.partial(body, mesh.shape["row"], mesh.shape["col"]),
        mesh=mesh,
        in_specs=(split, split) + (P(),) * 10,
        out_specs=(split, P(), P(), P()),
        check_vma=False,
    )
```

```python
import functools

import jax
import jax.numpy as jnp
from jax import lax
from jax.experimental import pallas as pl
from jax.experimental.pallas import tpu as pltpu
from jax.sharding import PartitionSpec as P

EPS = 1e-05
MESH = pl.DeviceIdType.MESH
F32 = jnp.float32
BF16 = jnp.bfloat16
LANES = 128
WIDE = 2


def dot(left, right, dims):
    return lax.dot_general(left, right, ((dims[:1], dims[1:]), ((), ())), preferred_element_type=F32)


def mean(values):
    return jnp.mean(values, axis=-1, keepdims=True)


def normalise(values):
    centred = values - mean(values)
    inverse = lax.rsqrt(mean(centred * centred) + EPS)
    return centred * inverse, inverse


def norm_back(grad, normed, inverse):
    return (grad - mean(grad) - normed * mean(grad * normed)) * inverse


def unfold(values, rows):
    parts = values.reshape(-1, 16, LANES)
    return jnp.concatenate([parts[:, :, :rows], parts[:, :, rows:]], axis=1).reshape(-1, rows)


def fold(values, rows):
    parts = values.reshape(-1, 32, rows)
    return jnp.concatenate([parts[:, :16], parts[:, 16:]], axis=2).reshape(-1, LANES)


def kernel(
    nr, nc, rows, cols,
    pair, cot, mask_s, chain_s, mask_v, chain_v, gain_in, bias_in, w_proj, w_gate, chain_bias,
    gain_out, bias_out, w_out,
    out, out_proj, out_gate, out_out,
    in32, cot32, zn_s, normed_s, inv_s, act_s, gate_s, q_s, mid_s, gu_s, gz_s,
    fold_a, fold_b, big32, a_mats, b_mats, g_mats,
    a_send, a_recv, b_send, b_all, m_send, m_recv, g_send, g_recv, ga_send, ga_recv,
    gp_send, gp_recv, gb_send, gb_recv, acc, w_send, w_recv, r_recv, f_recv,
    send_sem, recv_sem, bs_sem, br_sem, ps_sem, pr_sem, rs_sem, rr_sem,
):
    r = lax.axis_index("row")
    c = lax.axis_index("col")
    total = nr * rows
    hc = LANES // nc
    hq = 8
    nh = hc // hq
    slab = 16 * hq
    part = nc * slab
    full = nh * part
    lines = nc * 16

    def mod(value, count):
        return lax.rem(value + count, count)

    def span(start, size):
        return pl.ds(pl.multiple_of(start, 16), size)

    def at(ref, start, size):
        return ref.at[span(start, size)]

    barrier = pltpu.get_barrier_semaphore()
    for o in range(1, nc):
        pl.semaphore_signal(barrier, inc=1, device_id=(r, mod(c + o, nc)), device_id_type=MESH)
    for o in range(1, nr):
        pl.semaphore_signal(barrier, inc=1, device_id=(mod(r + o, nr), c), device_id_type=MESH)

    def col_copy(which, o, src, dst):
        return pltpu.make_async_remote_copy(
            src_ref=src, dst_ref=dst, send_sem=send_sem.at[which, o], recv_sem=recv_sem.at[which, o],
            device_id=(r, mod(c + o, nc)), device_id_type=MESH)

    def scatter(which, src, dst, first=0, base=0, size=slab):
        for o in range(1, nc):
            col_copy(which, o, at(src, first + mod(c + o, nc) * size, size), at(dst, base + c * size, size)).start()
        dst[span(base + c * size, size), :] = src[span(first + c * size, size), :]

    def arrived(which, o, dst, base=0, size=slab):
        piece = at(dst, base + mod(c - o, nc) * size, size)
        col_copy(which, o, piece, piece).wait_recv()

    def gathered(which, dst, base=0, size=slab):
        for o in range(1, nc):
            arrived(which, o, dst, base, size)

    def cast(dst, src, count, start=0):
        size = 256
        def step(t, carry):
            piece = pl.ds(pl.multiple_of(start + t * size, 16), size)
            dst[piece, :] = src[piece, :].astype(dst.dtype)
            return carry
        lax.fori_loop(0, count // size, step, 0)

    def put_turned(dst, step, values):
        for w in range(WIDE):
            turned = values[w * LANES:(w + 1) * LANES].T
            for t in range(nc):
                for half in range(nh):
                    row = ((half * nc + t) * 16 + step * WIDE + w) * hq
                    first = t * hc + half * hq
                    dst[pl.ds(pl.multiple_of(row, 8), hq), :] = turned[first:first + hq]

    def get_turned(src, step):
        blocks = []
        for w in range(WIDE):
            pieces = []
            for t in range(nc):
                for half in range(nh):
                    row = ((half * nc + t) * 16 + step * WIDE + w) * hq
                    pieces.append(src[pl.ds(pl.multiple_of(row, 8), hq), :])
            blocks.append(jnp.concatenate(pieces, axis=0).T)
        return jnp.concatenate(blocks, axis=0)

    def natural(src, step):
        return jnp.concatenate(
            [src[pl.ds(step * WIDE + w + high, rows, stride=cols), :] for w in range(WIDE) for high in (0, 16)], axis=0)

    def here(step):
        return pl.ds(pl.multiple_of(step * WIDE * LANES, LANES), WIDE * LANES)

    def row_values(ref):
        shape = (rows, total)
        wanted = lax.broadcasted_iota(jnp.int32, shape, 0) + r * rows == lax.broadcasted_iota(jnp.int32, shape, 1)
        column = jnp.sum(jnp.where(wanted, ref[...].astype(F32), 0.0), axis=-1, keepdims=True)
        return jnp.concatenate([column] * (2 * WIDE), axis=0)

    position = lax.broadcasted_iota(jnp.int32, (WIDE * 2 * rows, 1), 0) // rows
    mask_rows = row_values(mask_v)
    chain_rows = row_values(chain_v)

    def col_values(ref, step):
        values = jnp.zeros(position.shape, F32)
        for w in range(WIDE):
            for high in range(2):
                scalar = ref[c * cols + step * WIDE + w + 16 * high].astype(F32)
                values = jnp.where(position == 2 * w + high, scalar, values)
        return values

    def pair_mask(step):
        return mask_rows * col_values(mask_s, step)

    def loop(step, count=16 // WIDE):
        def run(t, carry):
            step(t)
            return carry
        lax.fori_loop(0, count, run, 0)

    def activate(step, zn, first, dst):
        proj = dot(zn, w_proj[:, first:first + 2 * LANES], (1, 0))
        gate = jax.nn.sigmoid(proj[:, :LANES])
        value = proj[:, LANES:]
        act_s[here(step), first:first + LANES] = gate
        act_s[here(step), first + LANES:first + 2 * LANES] = value
        put_turned(dst, step, gate * value * pair_mask(step))

    cast(in32, pair, rows * cols)

    def project_b(step):
        normed, inverse = normalise(natural(in32, step))
        zn = (normed * gain_in[...] + bias_in[...]).astype(BF16)
        zn_s[here(step), :] = zn
        normed_s[here(step), :] = normed
        inv_s[here(step), :] = inverse
        activate(step, zn, 2 * LANES, fold_b)

    loop(project_b)
    cast(b_send, fold_b, full)
    pl.semaphore_wait(barrier, nc - 1 + nr - 1)

    def row_copy(sems, o, slot, src, dst):
        return pltpu.make_async_remote_copy(
            src_ref=src, dst_ref=dst, send_sem=sems[0].at[o, slot], recv_sem=sems[1].at[o, slot],
            device_id=(mod(r + o, nr), c), device_id_type=MESH)

    def which(array, half):
        return array * nh + half

    def spread(half, slot):
        piece = at(b_all, r * full + half * part + mod(c - slot, nc) * slab, slab)
        for o in range(1, nr):
            row_copy((bs_sem, br_sem), o, half * nc + slot, piece, piece).start()

    for half in range(nh):
        scatter(which(0, half), b_send, b_all, half * part, r * full + half * part)
        spread(half, 0)

    loop(lambda step: activate(step, zn_s[here(step), :], 0, fold_a))
    cast(a_send, fold_a, full)
    for half in range(nh):
        scatter(which(1, half), a_send, a_recv, half * part, half * part)
    for half in range(nh):
        for slot in range(1, nc):
            arrived(which(0, half), slot, b_all, r * full + half * part)
            spread(half, slot)

    cast(cot32, cot, rows * cols)

    def gates(step):
        same = (chain_rows == col_values(chain_s, step)).astype(F32)
        gate = jax.nn.sigmoid(dot(zn_s[here(step), :], w_gate[...], (1, 0)) + same * chain_bias[...])
        gate_s[here(step), :] = gate
        grad_update = (natural(cot32, step) * gate).astype(BF16)
        gu_s[here(step), :] = grad_update
        q_s[here(step), :] = dot(grad_update, w_out[...], (1, 1)) * gain_out[...]

    loop(gates)
    acc[...] = jnp.zeros_like(acc)

    for half in range(nh):
        gathered(which(1, half), a_recv, half * part)
        cast(fold_a, a_recv, part, half * part)
        for slot in range(nc):
            for o in range(1, nr):
                piece = at(b_all, mod(r - o, nr) * full + half * part + mod(c - slot, nc) * slab, slab)
                row_copy((bs_sem, br_sem), o, half * nc + slot, piece, piece).wait_recv()
        for t in range(nr):
            cast(big32, b_all, part, t * full + half * part)

        def mix(h):
            first = half * part + h
            a_mat = unfold(fold_a[pl.ds(first, lines, stride=hq), :], rows).astype(BF16)
            b_mat = jnp.concatenate(
                [unfold(big32[pl.ds(t * full + first, lines, stride=hq), :], rows) for t in range(nr)], axis=1
            ).astype(BF16)
            a_mats[half * hq + h] = a_mat
            b_mats[half * hq + h] = b_mat
            fold_b[pl.ds(first, lines, stride=hq), :] = fold(dot(a_mat, b_mat, (0, 0)).T, rows)

        loop(mix, hq)
        cast(m_send, fold_b, part, half * part)
        scatter(which(2, half), m_send, m_recv, half * part, half * part)

    for half in range(nh):
        gathered(which(2, half), m_recv, half * part)
        cast(fold_a, m_recv, part, half * part)

    def middle(step):
        normed, inverse = normalise(get_turned(fold_a, step))
        mid_s[here(step), :] = normed
        put_turned(fold_b, step, norm_back(q_s[here(step), :], normed, inverse))

    loop(middle)
    for half in range(nh):
        cast(g_send, fold_b, part, half * part)
        scatter(which(3, half), g_send, g_recv, half * part, half * part)

    def side_terms(step):
        y = (mid_s[here(step), :] * gain_out[...] + bias_out[...]).astype(BF16)
        update = dot(y, w_out[...], (1, 0))
        gate = gate_s[here(step), :]
        grad_logit = (natural(cot32, step) * update * gate * (1.0 - gate)).astype(BF16)
        acc[2 * LANES:3 * LANES, :] += dot(zn_s[here(step), :], grad_logit, (0, 0))
        acc[3 * LANES:4 * LANES, :] += dot(y, gu_s[here(step), :], (0, 0))
        gz_s[here(step), :] = dot(grad_logit, w_gate[...], (1, 1))

    loop(side_terms)

    for half in range(nh):
        gathered(which(3, half), g_recv, half * part)
        cast(fold_a, g_recv, part, half * part)

        def back_b(h):
            first = half * part + h
            g_mat = unfold(fold_a[pl.ds(first, lines, stride=hq), :], rows).astype(BF16)
            g_mats[half * hq + h] = g_mat
            grad = dot(a_mats[half * hq + h], g_mat, (1, 1))
            for t in range(nr):
                big32[pl.ds(t * full + first, lines, stride=hq), :] = fold(grad[:, t * rows:(t + 1) * rows], rows)

        loop(back_b, hq)
        for t in range(nr):
            cast(gp_send, big32, part, t * full + half * part)
        for slot in list(range(1, nc)) + [0]:
            for o in range(1, nr):
                src = at(gp_send, mod(r + o, nr) * full + half * part + mod(c + slot, nc) * slab, slab)
                dst = at(gp_recv, o * full + half * part + slot * slab, slab)
                row_copy((ps_sem, pr_sem), o, half * nc + slot, src, dst).start()

    for half in range(nh):
        def back_a(h):
            index = half * hq + h
            fold_b[pl.ds(half * part + h, lines, stride=hq), :] = fold(dot(b_mats[index], g_mats[index], (1, 0)), rows)

        loop(back_a, hq)
        cast(ga_send, fold_b, part, half * part)
        scatter(which(4, half), ga_send, ga_recv, half * part, half * part)

    def reduce(half):
        for slot in list(range(1, nc)) + [0]:
            target = half * part + mod(c + slot, nc) * slab
            summed = big32[span(r * full + target, slab), :]
            for o in range(1, nr):
                start = o * full + half * part + slot * slab
                row_copy((ps_sem, pr_sem), o, half * nc + slot, at(gp_recv, start, slab), at(gp_recv, start, slab)).wait_recv()
                summed = summed + gp_recv[start:start + slab, :].astype(F32)
            if slot == 0:
                gb_recv[span(target, slab), :] = summed.astype(BF16)
            else:
                gb_send[span(target, slab), :] = summed.astype(BF16)
                col_copy(which(5, half), slot, at(gb_send, target, slab), at(gb_recv, half * part + c * slab, slab)).start()

    def side(step, src, gate_at, block):
        masked = get_turned(src, step) * pair_mask(step)
        gate = act_s[here(step), gate_at:gate_at + LANES]
        value = act_s[here(step), gate_at + LANES:gate_at + 2 * LANES]
        value_grad = masked * gate
        grad_p = jnp.concatenate([value_grad * value * (1.0 - gate), value_grad], axis=1).astype(BF16)
        term = dot(zn_s[here(step), :], grad_p, (0, 0))
        acc[block * LANES:(block + 1) * LANES, :] += term[:, :LANES]
        acc[(block + 1) * LANES:(block + 2) * LANES, :] += term[:, LANES:]
        return gz_s[here(step), :] + dot(grad_p, w_proj[:, gate_at:gate_at + 2 * LANES], (1, 1))

    groups = ((0, 4 * LANES, 0), (4 * LANES, 2 * LANES, 1))

    def terms_out(group):
        first, size, index = groups[group]
        cast(w_send, acc, size, first)
        scatter(6 * nh + index, w_send, w_recv, first, first, size // nc)

    def terms_row(group):
        first, size, index = groups[group]
        share = size // nc
        gathered(6 * nh + index, w_recv, first, share)
        summed = w_recv[first:first + share, :].astype(F32)
        for t in range(1, nc):
            summed = summed + w_recv[first + t * share:first + (t + 1) * share, :].astype(F32)
        base = first // nc * nr
        r_recv[span(base + r * share, share), :] = summed.astype(BF16)
        for o in range(1, nr):
            piece = at(r_recv, base + r * share, share)
            row_copy((rs_sem, rr_sem), o, index, piece, piece).start()

    def terms_back(group):
        first, size, index = groups[group]
        share = size // nc
        base = first // nc * nr
        for o in range(1, nr):
            piece = at(r_recv, base + mod(r - o, nr) * share, share)
            row_copy((rs_sem, rr_sem), o, index, piece, piece).wait_recv()
        summed = r_recv[base:base + share, :].astype(F32)
        for t in range(1, nr):
            summed = summed + r_recv[base + t * share:base + (t + 1) * share, :].astype(F32)
        f_recv[span(first + c * share, share), :] = (summed * (1.0 / total)).astype(BF16)
        for o in range(1, nc):
            piece = at(f_recv, first + c * share, share)
            col_copy(6 * nh + 2 + index, o, piece, piece).start()

    def terms_in(group):
        first, size, index = groups[group]
        gathered(6 * nh + 2 + index, f_recv, first, size // nc)

    reduce(0)
    for half in range(nh):
        gathered(which(4, half), ga_recv, half * part)
        cast(fold_a, ga_recv, part, half * part)

    def finish_a(step):
        gz_s[here(step), :] = side(step, fold_a, 0, 0)

    loop(finish_a)
    for half in range(1, nh):
        reduce(half)
    terms_out(0)
    for half in range(nh):
        gathered(which(5, half), gb_recv, half * part)
        cast(fold_b, gb_recv, part, half * part)

    def finish_b(step):
        grad = side(step, fold_b, 2 * LANES, 4) * gain_in[...]
        result = norm_back(grad, normed_s[here(step), :], inv_s[here(step), :])
        for w in range(WIDE):
            for high in range(2):
                first = (2 * w + high) * rows
                in32[pl.ds(step * WIDE + w + 16 * high, rows, stride=cols), :] = result[first:first + rows]

    loop(finish_b)
    terms_out(1)
    terms_row(0)
    cast(out, in32, rows * cols)
    terms_row(1)
    terms_back(0)
    terms_back(1)
    terms_in(0)
    for t in range(2):
        out_proj[:, t * LANES:(t + 1) * LANES] = f_recv[t * LANES:(t + 1) * LANES, :].astype(F32)
    out_gate[...] = f_recv[2 * LANES:3 * LANES, :].astype(F32)
    out_out[...] = f_recv[3 * LANES:4 * LANES, :].astype(F32)
    terms_in(1)
    for t in range(2, 4):
        out_proj[:, t * LANES:(t + 1) * LANES] = f_recv[(t + 2) * LANES:(t + 3) * LANES, :].astype(F32)

    for o in range(1, nc):
        for array, ref in enumerate((b_send, a_send, m_send, g_send, ga_send, gb_send)):
            for half in range(nh):
                col_copy(which(array, half), o, at(ref, 0, slab), at(ref, 0, slab)).wait_send()
        for first, size, index in groups:
            piece = at(w_send, 0, size // nc)
            col_copy(6 * nh + index, o, piece, piece).wait_send()
            col_copy(6 * nh + 2 + index, o, piece, piece).wait_send()
    for o in range(1, nr):
        for slot in range(nh * nc):
            row_copy((bs_sem, br_sem), o, slot, at(b_all, 0, slab), at(b_all, 0, slab)).wait_send()
            row_copy((ps_sem, pr_sem), o, slot, at(gp_send, 0, slab), at(gp_send, 0, slab)).wait_send()
        for first, size, index in groups:
            piece = at(r_recv, 0, size // nc)
            row_copy((rs_sem, rr_sem), o, index, piece, piece).wait_send()


def body(
    nr, nc, pair, cotangent, res_mask, chain, ln_in_gain, ln_in_bias, w_proj, w_gate, chain_bias,
    ln_out_gain, ln_out_bias, w_out,
):
    rows, cols, width = pair.shape
    count = rows * cols
    total = nr * rows
    hc = LANES // nc
    halves = hc // 8
    full = LANES * 16
    share = 6 * LANES // nc
    vmem = pl.BlockSpec(memory_space=pltpu.VMEM)
    smem = pl.BlockSpec(memory_space=pltpu.SMEM)

    def wide(size, dtype=BF16):
        return pltpu.VMEM((size, LANES), dtype)

    scratch = [
        wide(count, F32), wide(count, F32), wide(count), wide(count, F32), pltpu.VMEM((count, 1), F32),
        pltpu.VMEM((count, 4 * LANES), F32), wide(count, F32), wide(count, F32), wide(count, F32), wide(count), wide(count, F32),
        wide(full, F32), wide(full, F32), wide(nr * full, F32),
        pltpu.VMEM((hc, total, rows), BF16), pltpu.VMEM((hc, total, total), BF16), pltpu.VMEM((hc, total, rows), BF16),
        wide(full), wide(full), wide(full), wide(nr * full), wide(full), wide(full), wide(full), wide(full), wide(full), wide(full),
        wide(nr * full), wide(nr * full), wide(full), wide(full), wide(6 * LANES, F32),
        wide(6 * LANES), wide(6 * LANES), wide(nr * share), wide(6 * LANES),
        pltpu.SemaphoreType.DMA((6 * halves + 4, nc)), pltpu.SemaphoreType.DMA((6 * halves + 4, nc)),
        pltpu.SemaphoreType.DMA((nr, halves * nc)), pltpu.SemaphoreType.DMA((nr, halves * nc)),
        pltpu.SemaphoreType.DMA((nr, halves * nc)), pltpu.SemaphoreType.DMA((nr, halves * nc)),
        pltpu.SemaphoreType.DMA((nr, 2)), pltpu.SemaphoreType.DMA((nr, 2)),
    ]
    row = lambda values: values.reshape(1, -1)
    grads = pl.pallas_call(
        functools.partial(kernel, nr, nc, rows, cols),
        out_shape=(
            jax.ShapeDtypeStruct((count, width), BF16),
            jax.ShapeDtypeStruct((width, 4 * LANES), F32),
            jax.ShapeDtypeStruct((width, width), F32),
            jax.ShapeDtypeStruct((LANES, width), F32),
        ),
        in_specs=[vmem, vmem, smem, smem] + [vmem] * 10,
        out_specs=(vmem,) * 4,
        scratch_shapes=scratch,
        compiler_params=pltpu.CompilerParams(collective_id=0, has_side_effects=True, vmem_limit_bytes=56 * 2**20),
        cost_estimate=pl.CostEstimate(flops=2 * 10**9, bytes_accessed=4 * 2**20, transcendentals=0),
    )(
        pair.reshape(count, width), cotangent.reshape(count, width), res_mask, chain,
        row(res_mask), row(chain), row(ln_in_gain), row(ln_in_bias), w_proj, w_gate,
        row(chain_bias), row(ln_out_gain), row(ln_out_bias), w_out,
    )
    return (grads[0].reshape(rows, cols, width),) + tuple(grads[1:])


def solution(mesh):
    split = P("row", "col", None)
    return jax.shard_map(
        functools.partial(body, mesh.shape["row"], mesh.shape["col"]),
        mesh=mesh,
        in_specs=(split, split) + (P(),) * 10,
        out_specs=(split, P(), P(), P()),
        check_vma=False,
    )
```

```python
import functools

import jax
import jax.numpy as jnp
from jax import lax
from jax.experimental import pallas as pl
from jax.experimental.pallas import tpu as pltpu
from jax.sharding import PartitionSpec as P

EPS = 1e-05
MESH = pl.DeviceIdType.MESH
F32 = jnp.float32
BF16 = jnp.bfloat16
LANES = 128
WIDE = 2


def dot(left, right, dims):
    return lax.dot_general(left, right, ((dims[:1], dims[1:]), ((), ())), preferred_element_type=F32)


def mean(values):
    return jnp.mean(values, axis=-1, keepdims=True)


def normalise(values):
    centred = values - mean(values)
    inverse = lax.rsqrt(mean(centred * centred) + EPS)
    return centred * inverse, inverse


def norm_back(grad, normed, inverse):
    return (grad - mean(grad) - normed * mean(grad * normed)) * inverse


def unfold(values, rows):
    parts = values.reshape(-1, 16, LANES)
    return jnp.concatenate([parts[:, :, :rows], parts[:, :, rows:]], axis=1).reshape(-1, rows)


def fold(values, rows):
    parts = values.reshape(-1, 32, rows)
    return jnp.concatenate([parts[:, :16], parts[:, 16:]], axis=2).reshape(-1, LANES)


def kernel(
    nr, nc, rows, cols,
    pair, cot, mask_s, chain_s, mask_v, chain_v, gain_in, bias_in, w_proj, w_gate, chain_bias,
    gain_out, bias_out, w_out,
    out, out_proj, out_gate, out_out,
    in32, cot32, zn_s, normed_s, inv_s, act_s, gate_s, q_s, mid_s, gu_s, gz_s,
    fold_a, fold_b, fold_c, a_mats, b_mats, g_mats,
    a_send, a_recv, b_send, b_recv, m_send, m_recv, g_send, g_recv, ga_send, ga_recv,
    gb_send, gb_recv, acc, w_send, w_recv, r_recv, f_recv,
    send_sem, recv_sem, ts_sem, tr_sem, rs_sem, rr_sem,
):
    r = lax.axis_index("row")
    c = lax.axis_index("col")
    total = nr * rows
    nd = nr * nc
    me = r * nc + c
    hq = LANES // nd
    slab = 16 * hq
    part = nc * slab
    full = nd * slab
    lines = nc * 16

    def mod(value, count):
        return lax.rem(value + count, count)

    def span(start, size):
        return pl.ds(pl.multiple_of(start, 16), size)

    def at(ref, start, size):
        return ref.at[span(start, size)]

    barrier = pltpu.get_barrier_semaphore()
    def peer(o):
        other = mod(me + o, nd)
        return (other // nc, other % nc)

    def greet(o, carry):
        pl.semaphore_signal(barrier, inc=1, device_id=peer(o), device_id_type=MESH)
        return carry

    lax.fori_loop(1, nd, greet, 0)

    def copy(array, o, src, dst):
        return pltpu.make_async_remote_copy(
            src_ref=src, dst_ref=dst, send_sem=send_sem.at[array, o], recv_sem=recv_sem.at[array, o],
            device_id=peer(o), device_id_type=MESH)

    def exchange(array, src, dst):
        def send(o, carry):
            copy(array, o, at(src, mod(me + o, nd) * slab, slab), at(dst, me * slab, slab)).start()
            return carry
        lax.fori_loop(1, nd, send, 0)
        dst[span(me * slab, slab), :] = src[span(me * slab, slab), :]

    def arrive(array, dst):
        def take(o, carry):
            piece = at(dst, mod(me - o, nd) * slab, slab)
            copy(array, o, piece, piece).wait_recv()
            return carry
        lax.fori_loop(1, nd, take, 0)

    def col_copy(which, o, src, dst):
        return pltpu.make_async_remote_copy(
            src_ref=src, dst_ref=dst, send_sem=ts_sem.at[which, o], recv_sem=tr_sem.at[which, o],
            device_id=(r, mod(c + o, nc)), device_id_type=MESH)

    def scatter(which, src, dst, first, base, size):
        for o in range(1, nc):
            col_copy(which, o, at(src, first + mod(c + o, nc) * size, size), at(dst, base + c * size, size)).start()
        dst[span(base + c * size, size), :] = src[span(first + c * size, size), :]

    def gathered(which, dst, base, size):
        for o in range(1, nc):
            piece = at(dst, base + mod(c - o, nc) * size, size)
            col_copy(which, o, piece, piece).wait_recv()

    def cast(dst, src, count, start=0):
        size = 256
        def step(t, carry):
            piece = pl.ds(pl.multiple_of(start + t * size, 16), size)
            dst[piece, :] = src[piece, :].astype(dst.dtype)
            return carry
        lax.fori_loop(0, count // size, step, 0)

    def put_turned(dst, step, values):
        turned = [values[w * LANES:(w + 1) * LANES].T for w in range(WIDE)]
        for t in range(nd):
            row = pl.multiple_of((t * 16 + step * WIDE) * hq, WIDE * hq)
            dst[pl.ds(row, WIDE * hq), :] = jnp.concatenate([block[t * hq:(t + 1) * hq] for block in turned], axis=0)

    def get_turned(src, step):
        pieces = [
            src[pl.ds(pl.multiple_of((t * 16 + step * WIDE) * hq, WIDE * hq), WIDE * hq), :] for t in range(nd)
        ]
        blocks = [jnp.concatenate([piece[w * hq:(w + 1) * hq] for piece in pieces], axis=0).T for w in range(WIDE)]
        return jnp.concatenate(blocks, axis=0)

    def matrix(src, h):
        return jnp.concatenate(
            [unfold(src[pl.ds(t * part + h, lines, stride=hq), :], rows) for t in range(nr)], axis=1).astype(BF16)

    def put_matrix(dst, h, values):
        for t in range(nr):
            dst[pl.ds(t * part + h, lines, stride=hq), :] = fold(values[:, t * rows:(t + 1) * rows], rows)

    def natural(src, step):
        return jnp.concatenate(
            [src[pl.ds(step * WIDE + w + high, rows, stride=cols), :] for w in range(WIDE) for high in (0, 16)], axis=0)

    def here(step):
        return pl.ds(pl.multiple_of(step * WIDE * LANES, LANES), WIDE * LANES)

    def row_values(ref):
        shape = (rows, total)
        wanted = lax.broadcasted_iota(jnp.int32, shape, 0) + r * rows == lax.broadcasted_iota(jnp.int32, shape, 1)
        column = jnp.sum(jnp.where(wanted, ref[...].astype(F32), 0.0), axis=-1, keepdims=True)
        return jnp.concatenate([column] * (2 * WIDE), axis=0)

    position = lax.broadcasted_iota(jnp.int32, (WIDE * 2 * rows, 1), 0) // rows
    mask_rows = row_values(mask_v)
    chain_rows = row_values(chain_v)

    def col_values(ref, step):
        values = jnp.zeros(position.shape, F32)
        for w in range(WIDE):
            for high in range(2):
                scalar = ref[c * cols + step * WIDE + w + 16 * high].astype(F32)
                values = jnp.where(position == 2 * w + high, scalar, values)
        return values

    def pair_mask(step):
        return mask_rows * col_values(mask_s, step)

    def loop(step, count=16 // WIDE):
        def run(t, carry):
            step(t)
            return carry
        lax.fori_loop(0, count, run, 0)

    def activate(step, zn, first, dst):
        proj = dot(zn, w_proj[:, first:first + 2 * LANES], (1, 0))
        gate = jax.nn.sigmoid(proj[:, :LANES])
        value = proj[:, LANES:]
        act_s[here(step), first:first + LANES] = gate
        act_s[here(step), first + LANES:first + 2 * LANES] = value
        put_turned(dst, step, gate * value * pair_mask(step))

    cast(in32, pair, rows * cols)

    def project_b(step):
        normed, inverse = normalise(natural(in32, step))
        zn = (normed * gain_in[...] + bias_in[...]).astype(BF16)
        zn_s[here(step), :] = zn
        normed_s[here(step), :] = normed
        inv_s[here(step), :] = inverse
        activate(step, zn, 2 * LANES, fold_b)

    loop(project_b)
    cast(b_send, fold_b, full)
    pl.semaphore_wait(barrier, nd - 1)

    exchange(0, b_send, b_recv)

    def row_copy(sems, o, slot, src, dst):
        return pltpu.make_async_remote_copy(
            src_ref=src, dst_ref=dst, send_sem=sems[0].at[o, slot], recv_sem=sems[1].at[o, slot],
            device_id=(mod(r + o, nr), c), device_id_type=MESH)

    loop(lambda step: activate(step, zn_s[here(step), :], 0, fold_a))
    cast(a_send, fold_a, full)
    exchange(1, a_send, a_recv)
    cast(cot32, cot, rows * cols)

    def gates(step):
        same = (chain_rows == col_values(chain_s, step)).astype(F32)
        gate = jax.nn.sigmoid(dot(zn_s[here(step), :], w_gate[...], (1, 0)) + same * chain_bias[...])
        gate_s[here(step), :] = gate
        grad_update = (natural(cot32, step) * gate).astype(BF16)
        gu_s[here(step), :] = grad_update
        q_s[here(step), :] = dot(grad_update, w_out[...], (1, 1)) * gain_out[...]

    loop(gates)
    acc[...] = jnp.zeros_like(acc)

    arrive(0, b_recv)
    cast(fold_b, b_recv, full)
    arrive(1, a_recv)
    cast(fold_a, a_recv, full)

    def mix(h):
        a_mat = matrix(fold_a, h)
        b_mat = matrix(fold_b, h)
        a_mats[h] = a_mat
        b_mats[h] = b_mat
        put_matrix(fold_c, h, dot(b_mat, a_mat, (0, 0)))

    loop(mix, hq)
    cast(m_send, fold_c, full)
    exchange(2, m_send, m_recv)
    arrive(2, m_recv)
    cast(fold_a, m_recv, full)

    def middle(step):
        normed, inverse = normalise(get_turned(fold_a, step))
        mid_s[here(step), :] = normed
        put_turned(fold_b, step, norm_back(q_s[here(step), :], normed, inverse))

    loop(middle)
    cast(g_send, fold_b, full)
    exchange(3, g_send, g_recv)

    def side_terms(step):
        y = (mid_s[here(step), :] * gain_out[...] + bias_out[...]).astype(BF16)
        update = dot(y, w_out[...], (1, 0))
        gate = gate_s[here(step), :]
        grad_logit = (natural(cot32, step) * update * gate * (1.0 - gate)).astype(BF16)
        acc[2 * LANES:3 * LANES, :] += dot(zn_s[here(step), :], grad_logit, (0, 0))
        acc[3 * LANES:4 * LANES, :] += dot(y, gu_s[here(step), :], (0, 0))
        gz_s[here(step), :] = dot(grad_logit, w_gate[...], (1, 1))

    loop(side_terms)

    arrive(3, g_recv)
    cast(fold_a, g_recv, full)

    def back_a(h):
        g_mat = matrix(fold_a, h)
        g_mats[h] = g_mat
        put_matrix(fold_c, h, dot(b_mats[h], g_mat, (1, 0)))

    loop(back_a, hq)
    cast(ga_send, fold_c, full)
    exchange(4, ga_send, ga_recv)
    loop(lambda h: put_matrix(fold_b, h, dot(a_mats[h], g_mats[h], (1, 1))), hq)
    cast(gb_send, fold_b, full)
    exchange(5, gb_send, gb_recv)

    def side(step, src, gate_at, block):
        masked = get_turned(src, step) * pair_mask(step)
        gate = act_s[here(step), gate_at:gate_at + LANES]
        value = act_s[here(step), gate_at + LANES:gate_at + 2 * LANES]
        value_grad = masked * gate
        grad_p = jnp.concatenate([value_grad * value * (1.0 - gate), value_grad], axis=1).astype(BF16)
        term = dot(zn_s[here(step), :], grad_p, (0, 0))
        acc[block * LANES:(block + 1) * LANES, :] += term[:, :LANES]
        acc[(block + 1) * LANES:(block + 2) * LANES, :] += term[:, LANES:]
        return gz_s[here(step), :] + dot(grad_p, w_proj[:, gate_at:gate_at + 2 * LANES], (1, 1))

    groups = ((0, 4 * LANES, 0), (4 * LANES, 2 * LANES, 1))

    def terms_out(group):
        first, size, index = groups[group]
        cast(w_send, acc, size, first)
        scatter(index, w_send, w_recv, first, first, size // nc)

    def terms_row(group):
        first, size, index = groups[group]
        share = size // nc
        gathered(index, w_recv, first, share)
        summed = w_recv[first:first + share, :].astype(F32)
        for t in range(1, nc):
            summed = summed + w_recv[first + t * share:first + (t + 1) * share, :].astype(F32)
        base = first // nc * nr
        r_recv[span(base + r * share, share), :] = summed.astype(BF16)
        for o in range(1, nr):
            piece = at(r_recv, base + r * share, share)
            row_copy((rs_sem, rr_sem), o, index, piece, piece).start()

    def terms_back(group):
        first, size, index = groups[group]
        share = size // nc
        base = first // nc * nr
        for o in range(1, nr):
            piece = at(r_recv, base + mod(r - o, nr) * share, share)
            row_copy((rs_sem, rr_sem), o, index, piece, piece).wait_recv()
        summed = r_recv[base:base + share, :].astype(F32)
        for t in range(1, nr):
            summed = summed + r_recv[base + t * share:base + (t + 1) * share, :].astype(F32)
        f_recv[span(first + c * share, share), :] = (summed * (1.0 / total)).astype(BF16)
        for o in range(1, nc):
            piece = at(f_recv, first + c * share, share)
            col_copy(2 + index, o, piece, piece).start()

    def terms_in(group):
        first, size, index = groups[group]
        gathered(2 + index, f_recv, first, size // nc)

    arrive(4, ga_recv)
    cast(fold_a, ga_recv, full)

    def finish_a(step):
        gz_s[here(step), :] = side(step, fold_a, 0, 0)

    loop(finish_a)
    terms_out(0)
    arrive(5, gb_recv)
    cast(fold_b, gb_recv, full)

    def finish_b(step):
        grad = side(step, fold_b, 2 * LANES, 4) * gain_in[...]
        result = norm_back(grad, normed_s[here(step), :], inv_s[here(step), :])
        for w in range(WIDE):
            for high in range(2):
                first = (2 * w + high) * rows
                in32[pl.ds(step * WIDE + w + 16 * high, rows, stride=cols), :] = result[first:first + rows]

    loop(finish_b)
    terms_out(1)
    terms_row(0)
    cast(out, in32, rows * cols)
    terms_row(1)
    terms_back(0)
    terms_back(1)
    terms_in(0)
    for t in range(2):
        out_proj[:, t * LANES:(t + 1) * LANES] = f_recv[t * LANES:(t + 1) * LANES, :].astype(F32)
    out_gate[...] = f_recv[2 * LANES:3 * LANES, :].astype(F32)
    out_out[...] = f_recv[3 * LANES:4 * LANES, :].astype(F32)
    terms_in(1)
    for t in range(2, 4):
        out_proj[:, t * LANES:(t + 1) * LANES] = f_recv[(t + 2) * LANES:(t + 3) * LANES, :].astype(F32)

    def sent(o, carry):
        for array, ref in enumerate((b_send, a_send, m_send, g_send, ga_send, gb_send)):
            copy(array, o, at(ref, 0, slab), at(ref, 0, slab)).wait_send()
        return carry

    lax.fori_loop(1, nd, sent, 0)
    for first, size, index in groups:
        for o in range(1, nc):
            piece = at(w_send, 0, size // nc)
            col_copy(index, o, piece, piece).wait_send()
            col_copy(2 + index, o, piece, piece).wait_send()
        for o in range(1, nr):
            piece = at(r_recv, 0, size // nc)
            row_copy((rs_sem, rr_sem), o, index, piece, piece).wait_send()


def body(
    nr, nc, pair, cotangent, res_mask, chain, ln_in_gain, ln_in_bias, w_proj, w_gate, chain_bias,
    ln_out_gain, ln_out_bias, w_out,
):
    rows, cols, width = pair.shape
    count = rows * cols
    total = nr * rows
    hq = LANES // (nr * nc)
    full = LANES * 16
    share = 6 * LANES // nc
    vmem = pl.BlockSpec(memory_space=pltpu.VMEM)
    smem = pl.BlockSpec(memory_space=pltpu.SMEM)

    def wide(size, dtype=BF16):
        return pltpu.VMEM((size, LANES), dtype)

    scratch = [
        wide(count, F32), wide(count, F32), wide(count), wide(count, F32), pltpu.VMEM((count, 1), F32),
        pltpu.VMEM((count, 4 * LANES), F32), wide(count, F32), wide(count, F32), wide(count, F32), wide(count), wide(count, F32),
        wide(full, F32), wide(full, F32), wide(full, F32),
        pltpu.VMEM((hq, total, total), BF16), pltpu.VMEM((hq, total, total), BF16), pltpu.VMEM((hq, total, total), BF16),
        wide(full), wide(full), wide(full), wide(full), wide(full), wide(full), wide(full), wide(full), wide(full), wide(full), wide(full), wide(full), wide(6 * LANES, F32),
        wide(6 * LANES), wide(6 * LANES), wide(nr * share), wide(6 * LANES),
        pltpu.SemaphoreType.DMA((6, nr * nc)), pltpu.SemaphoreType.DMA((6, nr * nc)),
        pltpu.SemaphoreType.DMA((4, nc)), pltpu.SemaphoreType.DMA((4, nc)),
        pltpu.SemaphoreType.DMA((nr, 2)), pltpu.SemaphoreType.DMA((nr, 2)),
    ]
    row = lambda values: values.reshape(1, -1)
    grads = pl.pallas_call(
        functools.partial(kernel, nr, nc, rows, cols),
        out_shape=(
            jax.ShapeDtypeStruct((count, width), BF16),
            jax.ShapeDtypeStruct((width, 4 * LANES), F32),
            jax.ShapeDtypeStruct((width, width), F32),
            jax.ShapeDtypeStruct((LANES, width), F32),
        ),
        in_specs=[vmem, vmem, smem, smem] + [vmem] * 10,
        out_specs=(vmem,) * 4,
        scratch_shapes=scratch,
        compiler_params=pltpu.CompilerParams(collective_id=0, has_side_effects=True, vmem_limit_bytes=56 * 2**20),
        cost_estimate=pl.CostEstimate(flops=2 * 10**9, bytes_accessed=4 * 2**20, transcendentals=0),
    )(
        pair.reshape(count, width), cotangent.reshape(count, width), res_mask, chain,
        row(res_mask), row(chain), row(ln_in_gain), row(ln_in_bias), w_proj, w_gate,
        row(chain_bias), row(ln_out_gain), row(ln_out_bias), w_out,
    )
    return (grads[0].reshape(rows, cols, width),) + tuple(grads[1:])


def solution(mesh):
    split = P("row", "col", None)
    return jax.shard_map(
        functools.partial(body, mesh.shape["row"], mesh.shape["col"]),
        mesh=mesh,
        in_specs=(split, split) + (P(),) * 10,
        out_specs=(split, P(), P(), P()),
        check_vma=False,
    )
```

```python
import functools

import jax
import jax.numpy as jnp
from jax import lax
from jax.experimental import pallas as pl
from jax.experimental.pallas import tpu as pltpu
from jax.sharding import PartitionSpec as P

EPS = 1e-05
MESH = pl.DeviceIdType.MESH
F32 = jnp.float32
BF16 = jnp.bfloat16
LANES = 128
WIDE = 4


def dot(left, right, dims):
    return lax.dot_general(left, right, ((dims[:1], dims[1:]), ((), ())), preferred_element_type=F32)


def mean(values):
    return jnp.mean(values, axis=-1, keepdims=True)


def normalise(values):
    centred = values - mean(values)
    inverse = lax.rsqrt(mean(centred * centred) + EPS)
    return centred * inverse, inverse


def norm_back(grad, normed, inverse):
    return (grad - mean(grad) - normed * mean(grad * normed)) * inverse


def unfold(values, rows):
    parts = values.reshape(-1, 16, LANES)
    return jnp.concatenate([parts[:, :, :rows], parts[:, :, rows:]], axis=1).reshape(-1, rows)


def fold(values, rows):
    parts = values.reshape(-1, 32, rows)
    return jnp.concatenate([parts[:, :16], parts[:, 16:]], axis=2).reshape(-1, LANES)


def kernel(
    nr, nc, rows, cols,
    pair, cot, mask_s, chain_s, mask_v, chain_v, gain_in, bias_in, w_proj, w_gate, chain_bias,
    gain_out, bias_out, w_out,
    out, out_proj, out_gate, out_out,
    in32, cot32, zn_s, normed_s, inv_s, act_s, gate_s, q_s, mid_s, gu_s, gz_s,
    fold_a, fold_b, fold_c, a_mats, b_mats, g_mats,
    a_send, a_recv, b_send, b_recv, m_send, m_recv, g_send, g_recv, ga_send, ga_recv,
    gb_send, gb_recv, acc, w_send, w_recv, r_recv, f_recv,
    send_sem, recv_sem, ts_sem, tr_sem, rs_sem, rr_sem,
):
    r = lax.axis_index("row")
    c = lax.axis_index("col")
    total = nr * rows
    nd = nr * nc
    me = r * nc + c
    hq = LANES // nd
    slab = 16 * hq
    part = nc * slab
    full = nd * slab
    lines = nc * 16

    def mod(value, count):
        return lax.rem(value + count, count)

    def span(start, size):
        return pl.ds(pl.multiple_of(start, 16), size)

    def at(ref, start, size):
        return ref.at[span(start, size)]

    barrier = pltpu.get_barrier_semaphore()
    def peer(o):
        other = mod(me + o, nd)
        return (other // nc, other % nc)

    def greet(o, carry):
        pl.semaphore_signal(barrier, inc=1, device_id=peer(o), device_id_type=MESH)
        return carry

    lax.fori_loop(1, nd, greet, 0)

    def copy(array, o, src, dst):
        return pltpu.make_async_remote_copy(
            src_ref=src, dst_ref=dst, send_sem=send_sem.at[array, o], recv_sem=recv_sem.at[array, o],
            device_id=peer(o), device_id_type=MESH)

    def exchange(array, src, dst):
        def send(o, carry):
            copy(array, o, at(src, mod(me + o, nd) * slab, slab), at(dst, me * slab, slab)).start()
            return carry
        lax.fori_loop(1, nd, send, 0)
        dst[span(me * slab, slab), :] = src[span(me * slab, slab), :]

    def arrive(array, dst):
        def take(o, carry):
            piece = at(dst, mod(me - o, nd) * slab, slab)
            copy(array, o, piece, piece).wait_recv()
            return carry
        lax.fori_loop(1, nd, take, 0)

    def col_copy(which, o, src, dst):
        return pltpu.make_async_remote_copy(
            src_ref=src, dst_ref=dst, send_sem=ts_sem.at[which, o], recv_sem=tr_sem.at[which, o],
            device_id=(r, mod(c + o, nc)), device_id_type=MESH)

    def scatter(which, src, dst, first, base, size):
        for o in range(1, nc):
            col_copy(which, o, at(src, first + mod(c + o, nc) * size, size), at(dst, base + c * size, size)).start()
        dst[span(base + c * size, size), :] = src[span(first + c * size, size), :]

    def gathered(which, dst, base, size):
        for o in range(1, nc):
            piece = at(dst, base + mod(c - o, nc) * size, size)
            col_copy(which, o, piece, piece).wait_recv()

    def cast(dst, src, count, start=0):
        size = 256
        def step(t, carry):
            piece = pl.ds(pl.multiple_of(start + t * size, 16), size)
            dst[piece, :] = src[piece, :].astype(dst.dtype)
            return carry
        lax.fori_loop(0, count // size, step, 0)

    def put_turned(dst, step, values):
        turned = [values[w * LANES:(w + 1) * LANES].T for w in range(WIDE)]
        for t in range(nd):
            row = pl.multiple_of((t * 16 + step * WIDE) * hq, WIDE * hq)
            dst[pl.ds(row, WIDE * hq), :] = jnp.concatenate([block[t * hq:(t + 1) * hq] for block in turned], axis=0)

    def get_turned(src, step):
        pieces = [
            src[pl.ds(pl.multiple_of((t * 16 + step * WIDE) * hq, WIDE * hq), WIDE * hq), :] for t in range(nd)
        ]
        blocks = [jnp.concatenate([piece[w * hq:(w + 1) * hq] for piece in pieces], axis=0).T for w in range(WIDE)]
        return jnp.concatenate(blocks, axis=0)

    def matrix(src, h):
        return jnp.concatenate(
            [unfold(src[pl.ds(t * part + h, lines, stride=hq), :], rows) for t in range(nr)], axis=1).astype(BF16)

    def put_matrix(dst, h, values):
        for t in range(nr):
            dst[pl.ds(t * part + h, lines, stride=hq), :] = fold(values[:, t * rows:(t + 1) * rows], rows)

    def natural(src, step):
        return jnp.concatenate(
            [src[pl.ds(step * WIDE + w + high, rows, stride=cols), :] for w in range(WIDE) for high in (0, 16)], axis=0)

    def here(step):
        return pl.ds(pl.multiple_of(step * WIDE * LANES, LANES), WIDE * LANES)

    def row_values(ref):
        shape = (rows, total)
        wanted = lax.broadcasted_iota(jnp.int32, shape, 0) + r * rows == lax.broadcasted_iota(jnp.int32, shape, 1)
        column = jnp.sum(jnp.where(wanted, ref[...].astype(F32), 0.0), axis=-1, keepdims=True)
        return jnp.concatenate([column] * (2 * WIDE), axis=0)

    position = lax.broadcasted_iota(jnp.int32, (WIDE * 2 * rows, 1), 0) // rows
    mask_rows = row_values(mask_v)
    chain_rows = row_values(chain_v)

    def col_values(ref, step):
        values = jnp.zeros(position.shape, F32)
        for w in range(WIDE):
            for high in range(2):
                scalar = ref[c * cols + step * WIDE + w + 16 * high].astype(F32)
                values = jnp.where(position == 2 * w + high, scalar, values)
        return values

    def pair_mask(step):
        return mask_rows * col_values(mask_s, step)

    def loop(step, count=16 // WIDE, unroll=1):
        def run(t, carry):
            step(t)
            return carry
        lax.fori_loop(0, count, run, 0, unroll=unroll)

    def activate(step, zn, first, dst):
        proj = dot(zn, w_proj[:, first:first + 2 * LANES], (1, 0))
        gate = jax.nn.sigmoid(proj[:, :LANES])
        value = proj[:, LANES:]
        act_s[here(step), first:first + LANES] = gate
        act_s[here(step), first + LANES:first + 2 * LANES] = value
        put_turned(dst, step, gate * value * pair_mask(step))

    cast(in32, pair, rows * cols)

    def project_b(step):
        normed, inverse = normalise(natural(in32, step))
        zn = (normed * gain_in[...] + bias_in[...]).astype(BF16)
        zn_s[here(step), :] = zn
        normed_s[here(step), :] = normed
        inv_s[here(step), :] = inverse
        activate(step, zn, 2 * LANES, fold_b)

    loop(project_b)
    cast(b_send, fold_b, full)
    pl.semaphore_wait(barrier, nd - 1)

    exchange(0, b_send, b_recv)

    def row_copy(sems, o, slot, src, dst):
        return pltpu.make_async_remote_copy(
            src_ref=src, dst_ref=dst, send_sem=sems[0].at[o, slot], recv_sem=sems[1].at[o, slot],
            device_id=(mod(r + o, nr), c), device_id_type=MESH)

    loop(lambda step: activate(step, zn_s[here(step), :], 0, fold_a))
    cast(a_send, fold_a, full)
    exchange(1, a_send, a_recv)
    cast(cot32, cot, rows * cols)

    def gates(step):
        same = (chain_rows == col_values(chain_s, step)).astype(F32)
        gate = jax.nn.sigmoid(dot(zn_s[here(step), :], w_gate[...], (1, 0)) + same * chain_bias[...])
        gate_s[here(step), :] = gate
        grad_update = (natural(cot32, step) * gate).astype(BF16)
        gu_s[here(step), :] = grad_update
        q_s[here(step), :] = dot(grad_update, w_out[...], (1, 1)) * gain_out[...]

    loop(gates)
    acc[...] = jnp.zeros_like(acc)

    arrive(0, b_recv)
    cast(fold_b, b_recv, full)
    arrive(1, a_recv)
    cast(fold_a, a_recv, full)

    def mix(h):
        a_mat = matrix(fold_a, h)
        b_mat = matrix(fold_b, h)
        a_mats[h] = a_mat
        b_mats[h] = b_mat
        put_matrix(fold_c, h, dot(b_mat, a_mat, (0, 0)))

    loop(mix, hq, min(hq, 4))
    cast(m_send, fold_c, full)
    exchange(2, m_send, m_recv)
    arrive(2, m_recv)
    cast(fold_a, m_recv, full)

    def middle(step):
        normed, inverse = normalise(get_turned(fold_a, step))
        mid_s[here(step), :] = normed
        put_turned(fold_b, step, norm_back(q_s[here(step), :], normed, inverse))

    loop(middle)
    cast(g_send, fold_b, full)
    exchange(3, g_send, g_recv)

    def side_terms(step):
        y = (mid_s[here(step), :] * gain_out[...] + bias_out[...]).astype(BF16)
        update = dot(y, w_out[...], (1, 0))
        gate = gate_s[here(step), :]
        grad_logit = (natural(cot32, step) * update * gate * (1.0 - gate)).astype(BF16)
        acc[2 * LANES:3 * LANES, :] += dot(zn_s[here(step), :], grad_logit, (0, 0))
        acc[3 * LANES:4 * LANES, :] += dot(y, gu_s[here(step), :], (0, 0))
        gz_s[here(step), :] = dot(grad_logit, w_gate[...], (1, 1))

    loop(side_terms)

    arrive(3, g_recv)
    cast(fold_a, g_recv, full)

    def back_a(h):
        g_mat = matrix(fold_a, h)
        g_mats[h] = g_mat
        put_matrix(fold_c, h, dot(b_mats[h], g_mat, (1, 0)))

    loop(back_a, hq, min(hq, 4))
    cast(ga_send, fold_c, full)
    exchange(4, ga_send, ga_recv)
    loop(lambda h: put_matrix(fold_b, h, dot(a_mats[h], g_mats[h], (1, 1))), hq, min(hq, 4))
    cast(gb_send, fold_b, full)
    exchange(5, gb_send, gb_recv)

    def side(step, src, gate_at, block):
        masked = get_turned(src, step) * pair_mask(step)
        gate = act_s[here(step), gate_at:gate_at + LANES]
        value = act_s[here(step), gate_at + LANES:gate_at + 2 * LANES]
        value_grad = masked * gate
        grad_p = jnp.concatenate([value_grad * value * (1.0 - gate), value_grad], axis=1).astype(BF16)
        term = dot(zn_s[here(step), :], grad_p, (0, 0))
        acc[block * LANES:(block + 1) * LANES, :] += term[:, :LANES]
        acc[(block + 1) * LANES:(block + 2) * LANES, :] += term[:, LANES:]
        return gz_s[here(step), :] + dot(grad_p, w_proj[:, gate_at:gate_at + 2 * LANES], (1, 1))

    groups = ((0, 4 * LANES, 0), (4 * LANES, 2 * LANES, 1))

    def terms_out(group):
        first, size, index = groups[group]
        cast(w_send, acc, size, first)
        scatter(index, w_send, w_recv, first, first, size // nc)

    def terms_row(group):
        first, size, index = groups[group]
        share = size // nc
        gathered(index, w_recv, first, share)
        summed = w_recv[first:first + share, :].astype(F32)
        for t in range(1, nc):
            summed = summed + w_recv[first + t * share:first + (t + 1) * share, :].astype(F32)
        base = first // nc * nr
        r_recv[span(base + r * share, share), :] = summed.astype(BF16)
        for o in range(1, nr):
            piece = at(r_recv, base + r * share, share)
            row_copy((rs_sem, rr_sem), o, index, piece, piece).start()

    def terms_back(group):
        first, size, index = groups[group]
        share = size // nc
        base = first // nc * nr
        for o in range(1, nr):
            piece = at(r_recv, base + mod(r - o, nr) * share, share)
            row_copy((rs_sem, rr_sem), o, index, piece, piece).wait_recv()
        summed = r_recv[base:base + share, :].astype(F32)
        for t in range(1, nr):
            summed = summed + r_recv[base + t * share:base + (t + 1) * share, :].astype(F32)
        f_recv[span(first + c * share, share), :] = (summed * (1.0 / total)).astype(BF16)
        for o in range(1, nc):
            piece = at(f_recv, first + c * share, share)
            col_copy(2 + index, o, piece, piece).start()

    def terms_in(group):
        first, size, index = groups[group]
        gathered(2 + index, f_recv, first, size // nc)

    arrive(4, ga_recv)
    cast(fold_a, ga_recv, full)

    def finish_a(step):
        gz_s[here(step), :] = side(step, fold_a, 0, 0)

    loop(finish_a)
    terms_out(0)
    arrive(5, gb_recv)
    cast(fold_b, gb_recv, full)

    def finish_b(step):
        grad = side(step, fold_b, 2 * LANES, 4) * gain_in[...]
        result = norm_back(grad, normed_s[here(step), :], inv_s[here(step), :])
        for w in range(WIDE):
            for high in range(2):
                first = (2 * w + high) * rows
                out[pl.ds(step * WIDE + w + 16 * high, rows, stride=cols), :] = result[first:first + rows]

    loop(finish_b)
    terms_out(1)
    terms_row(0)
    terms_row(1)
    terms_back(0)
    terms_back(1)
    terms_in(0)
    for t in range(2):
        out_proj[:, t * LANES:(t + 1) * LANES] = f_recv[t * LANES:(t + 1) * LANES, :].astype(F32)
    out_gate[...] = f_recv[2 * LANES:3 * LANES, :].astype(F32)
    out_out[...] = f_recv[3 * LANES:4 * LANES, :].astype(F32)
    terms_in(1)
    for t in range(2, 4):
        out_proj[:, t * LANES:(t + 1) * LANES] = f_recv[(t + 2) * LANES:(t + 3) * LANES, :].astype(F32)

    def sent(o, carry):
        for array, ref in enumerate((b_send, a_send, m_send, g_send, ga_send, gb_send)):
            copy(array, o, at(ref, 0, slab), at(ref, 0, slab)).wait_send()
        return carry

    lax.fori_loop(1, nd, sent, 0)
    for first, size, index in groups:
        for o in range(1, nc):
            piece = at(w_send, 0, size // nc)
            col_copy(index, o, piece, piece).wait_send()
            col_copy(2 + index, o, piece, piece).wait_send()
        for o in range(1, nr):
            piece = at(r_recv, 0, size // nc)
            row_copy((rs_sem, rr_sem), o, index, piece, piece).wait_send()


def body(
    nr, nc, pair, cotangent, res_mask, chain, ln_in_gain, ln_in_bias, w_proj, w_gate, chain_bias,
    ln_out_gain, ln_out_bias, w_out,
):
    rows, cols, width = pair.shape
    count = rows * cols
    total = nr * rows
    hq = LANES // (nr * nc)
    full = LANES * 16
    share = 6 * LANES // nc
    vmem = pl.BlockSpec(memory_space=pltpu.VMEM)
    smem = pl.BlockSpec(memory_space=pltpu.SMEM)

    def wide(size, dtype=BF16):
        return pltpu.VMEM((size, LANES), dtype)

    scratch = [
        wide(count, F32), wide(count, F32), wide(count), wide(count, F32), pltpu.VMEM((count, 1), F32),
        pltpu.VMEM((count, 4 * LANES), F32), wide(count, F32), wide(count, F32), wide(count, F32), wide(count), wide(count, F32),
        wide(full, F32), wide(full, F32), wide(full, F32),
        pltpu.VMEM((hq, total, total), BF16), pltpu.VMEM((hq, total, total), BF16), pltpu.VMEM((hq, total, total), BF16),
        wide(full), wide(full), wide(full), wide(full), wide(full), wide(full), wide(full), wide(full), wide(full), wide(full), wide(full), wide(full), wide(6 * LANES, F32),
        wide(6 * LANES), wide(6 * LANES), wide(nr * share), wide(6 * LANES),
        pltpu.SemaphoreType.DMA((6, nr * nc)), pltpu.SemaphoreType.DMA((6, nr * nc)),
        pltpu.SemaphoreType.DMA((4, nc)), pltpu.SemaphoreType.DMA((4, nc)),
        pltpu.SemaphoreType.DMA((nr, 2)), pltpu.SemaphoreType.DMA((nr, 2)),
    ]
    row = lambda values: values.reshape(1, -1)
    grads = pl.pallas_call(
        functools.partial(kernel, nr, nc, rows, cols),
        out_shape=(
            jax.ShapeDtypeStruct((count, width), F32),
            jax.ShapeDtypeStruct((width, 4 * LANES), F32),
            jax.ShapeDtypeStruct((width, width), F32),
            jax.ShapeDtypeStruct((LANES, width), F32),
        ),
        in_specs=[vmem, vmem, smem, smem] + [vmem] * 10,
        out_specs=(vmem,) * 4,
        scratch_shapes=scratch,
        compiler_params=pltpu.CompilerParams(collective_id=0, has_side_effects=True, vmem_limit_bytes=56 * 2**20),
        cost_estimate=pl.CostEstimate(flops=2 * 10**9, bytes_accessed=4 * 2**20, transcendentals=0),
    )(
        pair.reshape(count, width), cotangent.reshape(count, width), res_mask, chain,
        row(res_mask), row(chain), row(ln_in_gain), row(ln_in_bias), w_proj, w_gate,
        row(chain_bias), row(ln_out_gain), row(ln_out_bias), w_out,
    )
    return (grads[0].astype(BF16).reshape(rows, cols, width),) + tuple(grads[1:])


def solution(mesh):
    split = P("row", "col", None)
    return jax.shard_map(
        functools.partial(body, mesh.shape["row"], mesh.shape["col"]),
        mesh=mesh,
        in_specs=(split, split) + (P(),) * 10,
        out_specs=(split, P(), P(), P()),
        check_vma=False,
    )
```
